256 devices in a mesh: blk: 16 (over x_lo, y, core), rep: 16 (over x_hi, z).
Axes of the slice: x: 4 (x_hi: 2, x_lo: 2; x = x_hi * 2 + x_lo), y: 4, z: 8, core: 2. Of those that a mesh axis runs over, the one named last changes fastest.
Arguments:
- tokens: bfloat16 [196608, 576], P(('blk', 'rep')), may hold values from -6 to 6
- cotangent: bfloat16 [196608, 576], P(('blk', 'rep')), may hold values from -16 to 16
- gate_up: bfloat16 [16, 576, 1536], P('blk'), may hold values from -0.25 to 0.25
- down_proj: bfloat16 [16, 768, 576], P('blk'), may hold values from -0.21875 to 0.21875
- norm_gain: float32 [16, 576], P('blk'), may hold values from 0.1 to 1.9
Outputs:
- token_grad: bfloat16 [196608, 576], P(('blk', 'rep'))
- gate_up_grad: float32 [16, 576, 1536], P('blk', 'rep')
- down_grad: float32 [16, 768, 576], P('blk', None, 'rep')
- gain_grad: float32 [16, 576], P('blk', 'rep')
The draws below stay inside these ranges and needn't reach their ends.
All inputs are finite; a program needn't handle non-finite values.
Results may differ from the reference program's by a relative error of at most 0.029.
Values may be sent and summed in bfloat16 or wider, within the bound.
No kernel may reach another device: no remote copies, remote signals or barrier semaphores. Data moves between devices by JAX's collectives and lax.ppermute only.
A program may use at most 128 MiB of HBM per device.

```python
import jax
import jax.numpy as jnp
from jax import lax

D = 576
HID = 768
STEPS = 2
TOK_DEV = 768
LAYERS = 16
TOKENS = 196608
N_BLK = 16
N_REP = 16


def spiked(array, stream_key, source, target, parts, factor):
    owner, partner = [(jnp.arange(array.shape[axis_at]) // (array.shape[axis_at] // parts)).reshape([-1 if axis == axis_at else 1 for axis in range(array.ndim)]) for axis_at in (source, target)]
    chosen = jax.random.permutation(stream_key, parts)[partner]
    strong = (owner == chosen) | (owner == (partner + parts // 2) % parts)
    return jnp.where(strong, factor * array, array)


def block_scale(own_key, shape, pieces, smallest, top_value):
    gain, own = 1.0, jax.random.fold_in(own_key, 6)
    for axis_at, blocks in pieces:
        heights = jnp.exp(jax.random.uniform(jax.random.fold_in(own, axis_at), (blocks,), jnp.float32, smallest / len(pieces), top_value / len(pieces)))
        gain = gain * jnp.repeat(heights, shape[axis_at] // blocks).reshape([-1 if axis == axis_at else 1 for axis in range(len(shape))])
    return gain


def scatter_about(key, dims, scale, bound, shards=(), kind=jnp.bfloat16):
    gain = block_scale(key, dims, shards, -0.22, 0.18) if shards else 1.0
    result = jax.random.normal(key, dims, jnp.float32) * scale * gain
    return jnp.minimum(jnp.maximum(result, -bound), bound).astype(kind)


def noise_with(own_key, shape, deviation, bound, split, heavy, kind=jnp.bfloat16):
    result = deviation * jax.random.normal(own_key, shape, jnp.float32)
    if split:
        result = result * block_scale(own_key, shape, split, -0.22, 0.18)
    return jnp.clip(spiked(result, jax.random.fold_in(own_key, 3), *heavy), -bound, bound).astype(kind)


def setup_inputs(seed: int = 0) -> dict:
    key_list = jax.random.split(jax.random.key(seed), 6)
    tokens = scatter_about(key_list[0], (TOKENS, D), 1.0, 6.0, ((0, 256),))
    cotangent = noise_with(key_list[1], (TOKENS, D), 1.0, 16.0, ((0, 256),), (0, 1, 64, 4.0))
    gate_up = scatter_about(key_list[2], (LAYERS, D, 2 * HID), D ** -0.5, 0.25, ((0, 16),))
    down_proj = scatter_about(key_list[3], (LAYERS, HID, D), HID ** -0.5, 0.21875, ((0, 16),))
    norm_gain = jnp.clip(1.0 + 0.18 * jax.random.normal(key_list[4], (LAYERS, D), jnp.float32), 0.1, 1.9)
    return dict(tokens=tokens, cotangent=cotangent, gate_up=gate_up, down_proj=down_proj, norm_gain=norm_gain)


epsilon = 1e-05

def norm_parts(hidden, norm_gain):
    floated = hidden.astype(jnp.float32)
    inverse = lax.rsqrt(lax.optimization_barrier(jnp.mean(floated * floated, axis=-1, keepdims=True)) + epsilon)
    normed = (floated * inverse * norm_gain).astype(jnp.bfloat16)
    return (floated, inverse, normed)

def layer_forward(hidden, gate_up, down_weight, norm_gain):
    floated, inverse, normed = norm_parts(hidden, norm_gain)
    projected = jnp.dot(normed, gate_up, preferred_element_type=jnp.float32)
    width = down_weight.shape[0]
    gate_part = projected[:, :width]
    up_part = projected[:, width:]
    activated = (gate_part * jax.nn.sigmoid(gate_part) * up_part).astype(jnp.bfloat16)
    return (floated + jnp.dot(activated, down_weight, preferred_element_type=jnp.float32)).astype(jnp.bfloat16)

def layer_backward(hidden, outgrad, gate_up, down_weight, norm_gain):
    floated, inverse, normed = norm_parts(hidden, norm_gain)
    projected = jnp.dot(normed, gate_up, preferred_element_type=jnp.float32)
    width = down_weight.shape[0]
    gate_part = projected[:, :width]
    up_part = projected[:, width:]
    sigmoid_part = jax.nn.sigmoid(gate_part)
    activated = (gate_part * sigmoid_part * up_part).astype(jnp.bfloat16)
    down_term = lax.dot_general(activated, outgrad, (((0,), (0,)), ((), ())), preferred_element_type=jnp.float32)
    act_grad = lax.dot_general(outgrad, down_weight, (((1,), (1,)), ((), ())), preferred_element_type=jnp.float32)
    gate_grad = act_grad * up_part * sigmoid_part * (1.0 + gate_part * (1.0 - sigmoid_part))
    up_grad = act_grad * gate_part * sigmoid_part
    mixed_grad = jnp.concatenate([gate_grad, up_grad], axis=1).astype(jnp.bfloat16)
    gate_up_term = lax.dot_general(normed, mixed_grad, (((0,), (0,)), ((), ())), preferred_element_type=jnp.float32)
    norm_grad = lax.dot_general(mixed_grad, gate_up, (((1,), (1,)), ((), ())), preferred_element_type=jnp.float32)
    gain_term = lax.optimization_barrier(jnp.sum(norm_grad * floated * inverse, axis=0))
    scaled = norm_grad * norm_gain
    inner = lax.optimization_barrier(jnp.mean(scaled * floated, axis=-1, keepdims=True))
    hidden_grad = (outgrad.astype(jnp.float32) + inverse * (scaled - floated * inverse * inverse * inner)).astype(jnp.bfloat16)
    return (hidden_grad, gate_up_term, down_term, gain_term)

def reference(tokens, cotangent, gate_up, down_proj, norm_gain):
    blocks = N_BLK * N_REP
    token_blocks = tokens.reshape(blocks, TOK_DEV, D)
    cot_blocks = cotangent.reshape(blocks, TOK_DEV, D)
    totals = (jnp.zeros(gate_up.shape, jnp.float32), jnp.zeros(down_proj.shape, jnp.float32), jnp.zeros(norm_gain.shape, jnp.float32))

    def visit(carried, inputs):
        index, hidden, outgrad = inputs
        start = index // N_REP
        states = []
        for cycle_step in range(STEPS):
            layer = (start + cycle_step) % N_BLK
            states.append(hidden)
            hidden = layer_forward(hidden, gate_up[layer], down_proj[layer], norm_gain[layer])
        gu_total, down_total, gain_total = carried
        for cycle_step in reversed(range(STEPS)):
            layer = (start + cycle_step) % N_BLK
            outgrad, gu_term, down_term, gain_term = layer_backward(states[cycle_step], outgrad, gate_up[layer], down_proj[layer], norm_gain[layer])
            gu_total = gu_total.at[layer].add(gu_term)
            down_total = down_total.at[layer].add(down_term)
            gain_total = gain_total.at[layer].add(gain_term)
        return ((gu_total, down_total, gain_total), outgrad)
    indices = jnp.arange(blocks, dtype=jnp.int32)
    totals, grads = lax.scan(visit, totals, (indices, token_blocks, cot_blocks))
    return (grads.reshape(TOKENS, D), totals[0], totals[1], totals[2])
```

```python
import functools

import jax
import jax.numpy as jnp
from jax import lax
from jax.experimental import pallas as pl
from jax.experimental.pallas import tpu as pltpu
from jax.sharding import PartitionSpec as P

CHUNKS = 2

epsilon = 1e-05
bf16 = jnp.bfloat16
f32 = jnp.float32


def dot(a, b, contract):
    return lax.dot_general(a, b, ((contract[0], contract[1]), ((), ())), preferred_element_type=f32)


def norm_parts(hidden, gain):
    floated = hidden.astype(f32)
    inverse = lax.rsqrt(jnp.mean(floated * floated, axis=-1, keepdims=True) + epsilon)
    return floated, inverse, (floated * inverse * gain).astype(bf16)


def project(normed, gate_up):
    projected = dot(normed, gate_up, ((1,), (0,)))
    width = gate_up.shape[1] // 2
    gate_part = projected[:, :width]
    up_part = projected[:, width:]
    sig = jax.nn.sigmoid(gate_part)
    silu = gate_part * sig
    slope = up_part * sig * (1.0 + gate_part * (1.0 - sig))
    return (silu * up_part).astype(bf16), slope, silu


def back_through_norm(norm_grad, floated, inverse, outgrad, gain):
    gain_term = jnp.sum(norm_grad * floated * inverse, axis=0, keepdims=True)
    scaled = norm_grad * gain
    inner = jnp.mean(scaled * floated, axis=-1, keepdims=True)
    in_grad = outgrad.astype(f32) + inverse * (scaled - floated * (inverse * inverse * inner))
    return in_grad.astype(bf16), gain_term


def forward_kernel(h_ref, gu_ref, dn_ref, gain_ref, next_ref, normed_ref, act_ref, slope_ref, silu_ref):
    floated, _, normed = norm_parts(h_ref[...], gain_ref[...])
    normed_ref[...] = normed
    activated, slope, silu = project(normed, gu_ref[...])
    act_ref[...] = activated
    slope_ref[...] = slope.astype(bf16)
    silu_ref[...] = silu.astype(bf16)
    next_ref[...] = (floated + dot(activated, dn_ref[...], ((1,), (0,)))).astype(bf16)


def turn_kernel(h_ref, out_ref, gu_ref, dn_ref, gain_ref, in_ref, normed_ref, act_ref, mixed_ref, gain_term_ref):
    floated, inverse, normed = norm_parts(h_ref[...], gain_ref[...])
    normed_ref[...] = normed
    activated, slope, silu = project(normed, gu_ref[...])
    act_ref[...] = activated
    act_grad = dot(out_ref[...], dn_ref[...], ((1,), (1,)))
    mixed = jnp.concatenate([(act_grad * slope).astype(bf16), (act_grad * silu).astype(bf16)], axis=1)
    mixed_ref[...] = mixed
    norm_grad = dot(mixed, gu_ref[...], ((1,), (1,)))
    in_ref[...], gain_term_ref[...] = back_through_norm(norm_grad, floated, inverse, out_ref[...], gain_ref[...])


def backward_kernel(h_ref, out_ref, slope_ref, silu_ref, gu_ref, dn_ref, gain_ref, in_ref, mixed_ref, gain_term_ref):
    act_grad = dot(out_ref[...], dn_ref[...], ((1,), (1,)))
    mixed = jnp.concatenate(
        [
            (act_grad * slope_ref[...].astype(f32)).astype(bf16),
            (act_grad * silu_ref[...].astype(f32)).astype(bf16),
        ],
        axis=1,
    )
    mixed_ref[...] = mixed
    norm_grad = dot(mixed, gu_ref[...], ((1,), (1,)))
    floated, inverse, _ = norm_parts(h_ref[...], gain_ref[...])
    in_ref[...], gain_term_ref[...] = back_through_norm(norm_grad, floated, inverse, out_ref[...], gain_ref[...])


def weight_kernel(count, *refs):
    lefts, rights, total_ref = refs[:count], refs[count : 2 * count], refs[2 * count]
    total = None
    for left, right in zip(lefts, rights):
        term = dot(left[...], right[...], ((0,), (0,)))
        total = term if total is None else total + term
    total_ref[...] = total.astype(bf16)


def call(kernel, outs, args, flops):
    moved = sum(a.size * a.dtype.itemsize for a in args) + sum(s.size * s.dtype.itemsize for s in outs)
    return pl.pallas_call(
        kernel,
        out_shape=outs,
        compiler_params=pltpu.CompilerParams(vmem_limit_bytes=56 * 2**20),
        cost_estimate=pl.CostEstimate(flops=flops, bytes_accessed=moved, transcendentals=0),
    )(*args)


def passed_along(x, axis, by):
    peers = lax.axis_size(axis)
    return lax.ppermute(x, axis, [(i, (i + by) % peers) for i in range(peers)])


def per_device(tokens, cotangent, gate_up, down_proj, norm_gain):
    gate_up, down, gain = gate_up[0], down_proj[0], norm_gain
    rows, width = tokens.shape
    hid = down.shape[0]
    size = rows // CHUNKS
    wide = lambda n, dtype=bf16: jax.ShapeDtypeStruct((size, n), dtype)
    row = jax.ShapeDtypeStruct((1, width), f32)
    unit = 2 * size * width * hid
    parts = [slice(i * size, (i + 1) * size) for i in range(CHUNKS)]
    first, sent, cots = [], [], []
    for part in parts:
        cots.append(passed_along(cotangent[part], "blk", 1))
        nxt, *kept = call(
            forward_kernel,
            [wide(width), wide(width), wide(hid), wide(hid), wide(hid)],
            (tokens[part], gate_up, down, gain),
            3 * unit,
        )
        first.append(kept)
        sent.append(passed_along(nxt, "blk", 1))
    turned, returned = [], []
    for hidden, cot in zip(sent, cots):
        in_grad, *kept = call(
            turn_kernel,
            [wide(width), wide(width), wide(hid), wide(2 * hid), row],
            (hidden, cot, gate_up, down, gain),
            5 * unit,
        )
        turned.append(kept)
        returned.append(passed_along(in_grad, "blk", -1))
    token_grads, mixed, gain_terms = [], [], [kept[3] for kept in turned]
    for part, out, kept in zip(parts, returned, first):
        token_grad, mixed_grad, gain_term = call(
            backward_kernel,
            [wide(width), wide(2 * hid), row],
            (tokens[part], out, kept[2], kept[3], gate_up, down, gain),
            3 * unit,
        )
        token_grads.append(token_grad)
        mixed.append(mixed_grad)
        gain_terms.append(gain_term)
    weight = functools.partial(weight_kernel, 2 * CHUNKS)
    (down_term,) = call(
        weight,
        [jax.ShapeDtypeStruct((width, hid), bf16)],
        (*cots, *returned, *[kept[1] for kept in turned], *[kept[1] for kept in first]),
        2 * CHUNKS * unit,
    )
    (gate_up_term,) = call(
        weight,
        [jax.ShapeDtypeStruct((width, 2 * hid), bf16)],
        (*[kept[0] for kept in turned], *[kept[0] for kept in first], *[kept[2] for kept in turned], *mixed),
        4 * CHUNKS * unit,
    )
    gain_sum = functools.reduce(jnp.add, gain_terms).astype(bf16)
    tail = jnp.pad(gain_sum, ((0, 15), (0, 2 * hid - width)))
    gate_up_term = jnp.concatenate([gate_up_term, tail], axis=0)
    gate_up_all, down_all = lax.psum((gate_up_term, down_term), "rep")
    share = width // lax.axis_size("rep")
    start = lax.axis_index("rep") * share
    gate_up_mine = lax.dynamic_slice_in_dim(gate_up_all, start, share, 0).astype(f32)
    down_mine = lax.dynamic_slice_in_dim(down_all, start, share, 0).astype(f32).T
    gain_mine = lax.dynamic_slice_in_dim(gate_up_all[width], start, share, 0).astype(f32)
    return jnp.concatenate(token_grads, axis=0), gate_up_mine[None], down_mine[None], gain_mine[None]


def solution(mesh):
    placed = (
        P(("blk", "rep"), None),
        P(("blk", "rep"), None),
        P("blk", None, None),
        P("blk", None, None),
        P("blk", None),
    )
    return jax.shard_map(
        per_device,
        mesh=mesh,
        in_specs=placed,
        out_specs=(
            P(("blk", "rep"), None),
            P("blk", "rep", None),
            P("blk", None, "rep"),
            P("blk", "rep"),
        ),
        check_vma=False,
    )
```

```python
import functools

import jax
import jax.numpy as jnp
from jax import lax
from jax.experimental import pallas as pl
from jax.experimental.pallas import tpu as pltpu
from jax.sharding import PartitionSpec as P

CUTS = (0, 512, 768)
LANES = 128

epsilon = 1e-05
bf16 = jnp.bfloat16
f32 = jnp.float32


def mul(a, b):
    return lax.dot_general(a, b, (((1,), (0,)), ((), ())), preferred_element_type=f32)


def mul_nt(a, b):
    return lax.dot_general(a, b, (((1,), (1,)), ((), ())), preferred_element_type=f32)


def column(row):
    return jnp.transpose(jnp.broadcast_to(row, (LANES, row.shape[1])))[:, :1]


def norm_parts(hidden):
    floated = hidden.astype(f32)
    inverse = lax.rsqrt(jnp.mean(floated * floated, axis=0, keepdims=True) + epsilon)
    return floated, inverse


def project(normed, gate_up_t):
    projected = mul(gate_up_t, normed)
    width = gate_up_t.shape[0] // 2
    gate_part = projected[:width]
    up_part = projected[width:]
    sig = jax.nn.sigmoid(gate_part)
    silu = gate_part * sig
    slope = up_part * sig * (1.0 + gate_part * (1.0 - sig))
    return (silu * up_part).astype(bf16), slope, silu


def back_through_norm(norm_grad, floated, inverse, outgrad, gain):
    product = norm_grad * floated * inverse
    size = product.shape[1]
    gain_term = functools.reduce(jnp.add, [product[:, i : i + LANES] for i in range(0, size, LANES)])
    scaled = norm_grad * gain
    inner = jnp.mean(scaled * floated, axis=0, keepdims=True)
    in_grad = outgrad.astype(f32) + inverse * (scaled - floated * (inverse * inverse * inner))
    return in_grad.astype(bf16), gain_term


def forward_kernel(span, first, *refs):
    tok_ref, gu_ref, dn_t_ref, gain_ref = refs[:4]
    next_ref, normed_ref, act_ref, slope_ref, silu_ref, *made = refs[4 if first else 5 :]
    if first:
        gu_t_ref, dn_ref = made
        gu_t_ref[...] = jnp.transpose(gu_ref[...])
        dn_ref[...] = jnp.transpose(dn_t_ref[...])
    else:
        gu_t_ref = gu_ref
    floated, inverse = norm_parts(tok_ref[:, span[0] : span[1]])
    normed = (floated * inverse * column(gain_ref[...])).astype(bf16)
    normed_ref[...] = normed
    activated, slope, silu = project(normed, gu_t_ref[...])
    act_ref[...] = activated
    slope_ref[...] = slope.astype(bf16)
    silu_ref[...] = silu.astype(bf16)
    next_ref[...] = (floated + mul(dn_t_ref[...], activated)).astype(bf16)


def turn_kernel(span, h_ref, out_ref, gu_t_ref, gu_ref, dn_ref, gain_ref, _, in_ref, normed_ref, act_ref, mixed_ref, term_ref):
    outgrad = out_ref[:, span[0] : span[1]]
    gain = column(gain_ref[...])
    floated, inverse = norm_parts(h_ref[...])
    normed = (floated * inverse * gain).astype(bf16)
    normed_ref[...] = normed
    activated, slope, silu = project(normed, gu_t_ref[...])
    act_ref[...] = activated
    act_grad = mul(dn_ref[...], outgrad)
    mixed = jnp.concatenate([(act_grad * slope).astype(bf16), (act_grad * silu).astype(bf16)], axis=0)
    mixed_ref[...] = mixed
    norm_grad = mul(gu_ref[...], mixed)
    in_ref[...], term_ref[...] = back_through_norm(norm_grad, floated, inverse, outgrad, gain)


def weight_kernel(spans, out_ref, *refs):
    count = len(spans)
    normed, mixed, acts, terms = [refs[i * count : (i + 1) * count] for i in range(4)]
    gu_ref, dn_ref, gain_ref = refs[4 * count :]
    gu_ref[...] = functools.reduce(jnp.add, [mul_nt(a[...], b[...]) for a, b in zip(normed, mixed)])
    dn_ref[...] = functools.reduce(jnp.add, [mul_nt(out_ref[:, lo:hi], a[...]) for (lo, hi), a in zip(spans, acts)])
    gain_ref[...] = functools.reduce(jnp.add, [t[...] for t in terms])


def backward_kernel(span, last, *refs):
    tok_ref, out_ref, slope_ref, silu_ref, normed_ref, act_ref, dn_ref, gu_ref, gain_ref = refs[:9]
    gu_sum_ref, dn_sum_ref, gain_sum_ref = refs[9:12]
    hid = dn_ref.shape[0]
    gain = column(gain_ref[...])
    outgrad = out_ref[...]
    act_grad = mul(dn_ref[...], outgrad)
    mixed = jnp.concatenate(
        [
            (act_grad * slope_ref[...].astype(f32)).astype(bf16),
            (act_grad * silu_ref[...].astype(f32)).astype(bf16),
        ],
        axis=0,
    )
    floated, inverse = norm_parts(tok_ref[:, span[0] : span[1]])
    norm_grad = mul(gu_ref[...], mixed)
    in_grad, term = back_through_norm(norm_grad, floated, inverse, outgrad, gain)
    gu_sum = gu_sum_ref[...] + mul_nt(normed_ref[...], mixed)
    dn_sum = dn_sum_ref[...] + mul_nt(outgrad, act_ref[...])
    gain_sum = gain_sum_ref[...] + term
    if last:
        before_ref, grad_ref, total_ref = refs[12:]
        grad_ref[:, : span[0]] = before_ref[...]
        grad_ref[:, span[0] : span[1]] = in_grad
        total_ref[:, : 2 * hid] = gu_sum.astype(bf16)
        total_ref[:, 2 * hid : 3 * hid] = dn_sum.astype(bf16)
        gain_col = jnp.sum(gain_sum, axis=1, keepdims=True)
        total_ref[:, 3 * hid :] = jnp.broadcast_to(gain_col, (gain_col.shape[0], 2 * LANES)).astype(bf16)
    else:
        in_ref, gu_out, dn_out, gain_out = refs[12:]
        in_ref[...] = in_grad
        gu_out[...] = gu_sum
        dn_out[...] = dn_sum
        gain_out[...] = gain_sum


def call(kernel, outs, args, aliases={}, kept=True):
    shaped = pltpu.VMEM if kept else jax.ShapeDtypeStruct
    inside = pl.BlockSpec(memory_space=pltpu.VMEM)
    return pl.pallas_call(
        kernel,
        out_shape=[shaped(shape, dtype) for shape, dtype in outs],
        in_specs=[inside] * len(args),
        out_specs=[inside] * len(outs),
        input_output_aliases=aliases,
        compiler_params=pltpu.CompilerParams(vmem_limit_bytes=24 * 2**20),
    )(*[pltpu.with_memory_space_constraint(a, pltpu.VMEM) for a in args])


def passed_along(x, axis, by):
    peers = lax.axis_size(axis)
    return lax.ppermute(x, axis, [(i, (i + by) % peers) for i in range(peers)])


def split_kernel(in_ref, gu_ref, dn_ref, gain_ref):
    wide, hid = gu_ref.shape[2], dn_ref.shape[2]
    gu_ref[...] = in_ref[:, :wide].astype(f32)[:, None, :]
    dn_ref[...] = in_ref[:, wide : wide + hid].astype(f32)[:, None, :]
    gains = in_ref[:, wide + hid : wide + hid + LANES].astype(f32)
    row = lax.broadcasted_iota(jnp.int32, gains.shape, 0)
    lane = lax.broadcasted_iota(jnp.int32, gains.shape, 1)
    gain_ref[...] = jnp.sum(jnp.where(row == lane, gains, 0.0), axis=0, keepdims=True)[:, : gain_ref.shape[1]]


def per_device(tokens, cotangent, gate_up, down_proj, norm_gain):
    tok, cot = tokens.T, cotangent.T
    gu, dn_t, gain = gate_up[0], down_proj[0].T, norm_gain
    width, rows = tok.shape
    hid = dn_t.shape[1]
    spans = list(zip(CUTS[:-1], CUTS[1:]))
    out = passed_along(cot, "blk", 1)
    kept, nexts, sent = [], [], []
    gu_t = dn = None
    for lo, hi in spans:
        n = hi - lo
        first = lo == 0
        shapes = [((width, n), bf16), ((width, n), bf16)] + [((hid, n), bf16)] * 3
        args = (tok, gu, dn_t, gain) if first else (tok, gu_t, dn_t, gain, out)
        if first:
            shapes += [((2 * hid, width), bf16), ((hid, width), bf16)]
        nxt, *parts = call(functools.partial(forward_kernel, (lo, hi), first), shapes, args)
        if first:
            *parts, gu_t, dn = parts
        kept.append(parts)
        nexts.append(nxt)
        sent.append(passed_along(nxt, "blk", 1))
    turned, returned = [], []
    after = nexts[-1]
    for (lo, hi), hidden in zip(spans, sent):
        n = hi - lo
        in_grad, *parts = call(
            functools.partial(turn_kernel, (lo, hi)),
            [((width, n), bf16)] * 2 + [((hid, n), bf16), ((2 * hid, n), bf16), ((width, LANES), f32)],
            (hidden, out, gu_t, gu, dn, gain, after),
        )
        after = in_grad
        turned.append(parts)
        returned.append(passed_along(in_grad, "blk", -1))
    sums_shape = [((width, 2 * hid), f32), ((width, hid), f32), ((width, LANES), f32)]
    sums = call(
        functools.partial(weight_kernel, spans),
        sums_shape,
        [out] + [part[i] for i in (0, 2, 1, 3) for part in turned],
    )
    before = None
    for (lo, hi), back, (normed, act, slope, silu) in zip(spans, returned, kept):
        last = hi == rows
        args = (tok, back, slope, silu, normed, act, dn, gu, gain, *sums)
        kernel = functools.partial(backward_kernel, (lo, hi), last)
        if last:
            shapes = [((width, rows), bf16), ((width, 3 * hid + 2 * LANES), bf16)]
            grad, total = call(kernel, shapes, (*args, before))
        else:
            before, *sums = call(
                kernel, [((width, hi - lo), bf16)] + sums_shape, args, {9: 1, 10: 2, 11: 3}
            )
    mine = lax.psum_scatter(total, "rep", scatter_dimension=0, tiled=True)
    mine = lax.optimization_barrier(mine)
    share = mine.shape[0]
    gu_mine, dn_mine, gain_mine = call(
        split_kernel, [((share, 1, 2 * hid), f32), ((share, 1, hid), f32), ((1, share), f32)], (mine,), kept=False
    )
    return grad.T, gu_mine.transpose(1, 0, 2), dn_mine.transpose(1, 2, 0), gain_mine


def solution(mesh):
    placed = (
        P(("blk", "rep"), None),
        P(("blk", "rep"), None),
        P("blk", None, None),
        P("blk", None, None),
        P("blk", None),
    )
    return jax.shard_map(
        per_device,
        mesh=mesh,
        in_specs=placed,
        out_specs=(
            P(("blk", "rep"), None),
            P("blk", "rep", None),
            P("blk", None, "rep"),
            P("blk", "rep"),
        ),
        check_vma=False,
    )
```

```python
import functools

import jax
import jax.numpy as jnp
from jax import lax
from jax.experimental import pallas as pl
from jax.experimental.pallas import tpu as pltpu
from jax.sharding import PartitionSpec as P

SPANS = ((0, 512), (512, 768))
LANES = 128
SHARE = 36
RING = 8
HALF = 656
SLOT = 1328
SHORT = SLOT - 2

epsilon = 1e-05
bf16 = jnp.bfloat16
f32 = jnp.float32


def mul(a, b):
    return lax.dot_general(a, b, (((1,), (0,)), ((), ())), preferred_element_type=f32)


def mul_nt(a, b):
    return lax.dot_general(a, b, (((1,), (1,)), ((), ())), preferred_element_type=f32)


def column(row):
    return jnp.transpose(jnp.broadcast_to(row, (LANES, row.shape[1])))[:, :1]


def norm_parts(hidden):
    floated = hidden.astype(f32)
    inverse = lax.rsqrt(jnp.mean(floated * floated, axis=0, keepdims=True) + epsilon)
    return floated, inverse


def project(normed, gate_up_t):
    projected = mul(gate_up_t, normed)
    width = gate_up_t.shape[0] // 2
    gate_part = projected[:width]
    up_part = projected[width:]
    sig = jax.nn.sigmoid(gate_part)
    silu = gate_part * sig
    slope = up_part * sig * (1.0 + gate_part * (1.0 - sig))
    return (silu * up_part).astype(bf16), slope, silu


def back_through_norm(norm_grad, floated, inverse, outgrad, gain):
    product = norm_grad * floated * inverse
    size = product.shape[1]
    gain_term = functools.reduce(jnp.add, [product[:, i : i + LANES] for i in range(0, size, LANES)])
    scaled = norm_grad * gain
    inner = jnp.mean(scaled * floated, axis=0, keepdims=True)
    in_grad = outgrad.astype(f32) + inverse * (scaled - floated * (inverse * inverse * inner))
    return in_grad.astype(bf16), gain_term


def forward_kernel(tok_ref, gu_ref, dn_t_ref, gain_ref, next_ref, normed_ref, act_ref, slope_ref, silu_ref, gu_t_ref, dn_ref):
    gu_t_ref[...] = jnp.transpose(gu_ref[...])
    dn_ref[...] = jnp.transpose(dn_t_ref[...])
    gain = column(gain_ref[...])
    for lo, hi in SPANS:
        floated, inverse = norm_parts(tok_ref[:, lo:hi])
        normed = (floated * inverse * gain).astype(bf16)
        normed_ref[:, lo:hi] = normed
        activated, slope, silu = project(normed, gu_t_ref[...])
        act_ref[:, lo:hi] = activated
        slope_ref[:, lo:hi] = slope.astype(bf16)
        silu_ref[:, lo:hi] = silu.astype(bf16)
        next_ref[:, lo:hi] = (floated + mul(dn_t_ref[...], activated)).astype(bf16)


def turn_kernel(span, h_ref, out_ref, gu_t_ref, gu_ref, dn_ref, gain_ref, _, in_ref, normed_ref, act_ref, mixed_ref, term_ref):
    outgrad = out_ref[:, span[0] : span[1]]
    gain = column(gain_ref[...])
    floated, inverse = norm_parts(h_ref[:, span[0] : span[1]])
    normed = (floated * inverse * gain).astype(bf16)
    normed_ref[...] = normed
    activated, slope, silu = project(normed, gu_t_ref[...])
    act_ref[...] = activated
    act_grad = mul(dn_ref[...], outgrad)
    mixed = jnp.concatenate([(act_grad * slope).astype(bf16), (act_grad * silu).astype(bf16)], axis=0)
    mixed_ref[...] = mixed
    norm_grad = mul(gu_ref[...], mixed)
    in_ref[...], term_ref[...] = back_through_norm(norm_grad, floated, inverse, outgrad, gain)


def weight_kernel(out_ref, *refs):
    count = len(SPANS)
    normed, mixed, acts, terms = [refs[i * count : (i + 1) * count] for i in range(4)]
    gu_ref, dn_ref, gain_ref = refs[4 * count :]
    gu_ref[...] = functools.reduce(jnp.add, [mul_nt(a[...], b[...]) for a, b in zip(normed, mixed)])
    dn_ref[...] = functools.reduce(jnp.add, [mul_nt(out_ref[:, lo:hi], a[...]) for (lo, hi), a in zip(SPANS, acts)])
    gain_ref[...] = functools.reduce(jnp.add, [t[...] for t in terms])


def fill_slots(slots_ref, staged_ref, total_ref, sems, gu_sum, dn_sum, gain_sum):
    gain_sum = jnp.broadcast_to(gain_sum, (gain_sum.shape[0], LANES))
    columns = [x[:, i : i + LANES] for x in (gu_sum, dn_sum) for i in range(0, x.shape[1], LANES)]
    tail = HALF - SHARE * len(columns)
    own = lax.broadcasted_iota(jnp.int32, (SHARE, LANES), 0) == lax.broadcasted_iota(jnp.int32, (SHARE, LANES), 1)
    top = lax.broadcasted_iota(jnp.int32, (tail, LANES), 0) == 0
    copies = []
    for place in range(RING):
        for half in range(2):
            first = (half * RING + place) * SHARE
            rows = slice(first, first + SHARE)
            at = place * SLOT + half * HALF
            for column_block in columns:
                slots_ref[at : at + SHARE] = column_block[rows]
                at += SHARE
            gains = jnp.sum(jnp.where(own, gain_sum[rows], 0.0), axis=0, keepdims=True)
            slots_ref[at : at + tail] = jnp.where(top, gains, 0.0)
        low = place * SLOT
        if place < RING - 1:
            slots_ref[low + 2 * HALF : low + SLOT] = jnp.zeros((SLOT - 2 * HALF, LANES), f32)
            high = low + SLOT
        else:
            high = low + 2 * HALF
        staged_ref[low:high] = slots_ref[low:high].astype(bf16)
        copy = pltpu.make_async_copy(staged_ref.at[low:high], total_ref.at[low:high], sems.at[place])
        copy.start()
        copies.append(copy)
    for copy in copies:
        copy.wait()


def touch_kernel(out_ref, next_ref, seen_ref):
    seen_ref[...] = out_ref[:16, :LANES] + next_ref[:16, :LANES]


def backward_kernel(span, last, *refs):
    tok_ref, out_ref, slope_ref, silu_ref, normed_ref, act_ref, dn_ref, gu_ref, gain_ref = refs[:9]
    part = (slice(None), slice(*span))
    gu_sum_ref, dn_sum_ref, gain_sum_ref = refs[9:12]
    hid = dn_ref.shape[0]
    gain = column(gain_ref[...])
    outgrad = out_ref[...]
    act_grad = mul(dn_ref[...], outgrad)
    mixed = jnp.concatenate(
        [
            (act_grad * slope_ref[part].astype(f32)).astype(bf16),
            (act_grad * silu_ref[part].astype(f32)).astype(bf16),
        ],
        axis=0,
    )
    floated, inverse = norm_parts(tok_ref[part])
    norm_grad = mul(gu_ref[...], mixed)
    in_grad, term = back_through_norm(norm_grad, floated, inverse, outgrad, gain)
    gu_sum = gu_sum_ref[...] + mul_nt(normed_ref[part], mixed)
    dn_sum = dn_sum_ref[...] + mul_nt(outgrad, act_ref[part])
    gain_sum = gain_sum_ref[...] + term
    if last:
        before_ref, grad_ref, total_ref, slots_ref, staged_ref, sems = refs[12:]
        grad_ref[:, : span[0]] = before_ref[...]
        grad_ref[:, span[0] : span[1]] = in_grad
        gain_sum = jnp.sum(gain_sum, axis=1, keepdims=True)
        fill_slots(slots_ref, staged_ref, total_ref, sems, gu_sum, dn_sum, gain_sum)
    else:
        in_ref, gu_out, dn_out, gain_out = refs[12:]
        in_ref[...] = in_grad
        gu_out[...] = gu_sum
        dn_out[...] = dn_sum
        gain_out[...] = gain_sum


def call(kernel, outs, args, aliases={}, kept=True, scratch=(), free=0):
    shaped = pltpu.VMEM if kept else jax.ShapeDtypeStruct
    inside = pl.BlockSpec(memory_space=pltpu.VMEM)
    held = len(outs) - free
    return pl.pallas_call(
        kernel,
        out_shape=[shaped(*o) for o in outs[:held]] + [jax.ShapeDtypeStruct(*o) for o in outs[held:]],
        in_specs=[inside] * len(args),
        out_specs=[inside] * held + [pl.BlockSpec(memory_space=pl.ANY)] * free,
        input_output_aliases=aliases,
        scratch_shapes=scratch,
        compiler_params=pltpu.CompilerParams(vmem_limit_bytes=28 * 2**20),
    )(*[pltpu.with_memory_space_constraint(a, pltpu.VMEM) for a in args])


def passed_along(x, axis, by):
    peers = lax.axis_size(axis)
    return lax.ppermute(x, axis, [(i, (i + by) % peers) for i in range(peers)])


def split_kernel(in_ref, other_ref, gu_ref, dn_ref, gain_ref):
    at = 0
    got = in_ref[...].astype(f32) + other_ref[...].astype(f32)
    for ref in (gu_ref, dn_ref):
        for i in range(0, ref.shape[2], LANES):
            ref[:, :, i : i + LANES] = got[at : at + SHARE][:, None, :]
            at += SHARE
    gain_ref[...] = got[at : at + 1, :SHARE]


def per_device(tokens, cotangent, gate_up, down_proj, norm_gain):
    tok, cot = tokens.T, cotangent.T
    gu, dn_t, gain = gate_up[0], down_proj[0].T, norm_gain
    width, rows = tok.shape
    hid = dn_t.shape[1]
    length = RING * SHORT
    out = passed_along(cot, "blk", 1)
    wide = [((n, rows), bf16) for n in (width, width, hid, hid, hid)]
    nxt, normed, act, slope, silu, gu_t, dn = call(
        forward_kernel, wide + [((2 * hid, width), bf16), ((hid, width), bf16)], (tok, gu, dn_t, gain)
    )
    hidden = passed_along(nxt, "blk", 1)
    turned, returned = [], []
    (after,) = call(touch_kernel, [((16, LANES), bf16)], (out, nxt))
    for lo, hi in SPANS:
        n = hi - lo
        in_grad, *parts = call(
            functools.partial(turn_kernel, (lo, hi)),
            [((width, n), bf16)] * 2 + [((hid, n), bf16), ((2 * hid, n), bf16), ((width, LANES), f32)],
            (hidden, out, gu_t, gu, dn, gain, after),
        )
        after = in_grad
        turned.append(parts)
        returned.append(passed_along(in_grad, "blk", -1))
    sums_shape = [((width, 2 * hid), f32), ((width, hid), f32), ((width, LANES), f32)]
    sums = call(
        weight_kernel,
        sums_shape,
        [out] + [part[i] for i in (0, 2, 1, 3) for part in turned],
    )
    before = None
    for (lo, hi), back in zip(SPANS, returned):
        last = hi == rows
        args = (tok, back, slope, silu, normed, act, dn, gu, gain, *sums)
        kernel = functools.partial(backward_kernel, (lo, hi), last)
        if last:
            shapes = [((width, rows), bf16), ((length, LANES), bf16)]
            scratch = [pltpu.VMEM((length, LANES), f32), pltpu.VMEM((length, LANES), bf16), pltpu.SemaphoreType.DMA((RING,))]
            grad, total = call(kernel, shapes, (*args, before), scratch=scratch, free=1)
        else:
            before, *sums = call(
                kernel, [((width, hi - lo), bf16)] + sums_shape, args, {9: 1, 10: 2, 11: 3}
            )
    rings = [[half * RING + place for place in range(RING)] for half in range(2)]
    share = lax.psum_scatter(total, "rep", scatter_dimension=0, axis_index_groups=rings, tiled=True)
    share = lax.optimization_barrier(share)
    at = lax.axis_index("rep")
    half, start = at // RING, (at % RING) * (SLOT - SHORT)
    theirs = lax.dynamic_slice_in_dim(share, start + (1 - half) * HALF, HALF, 0)
    theirs = lax.ppermute(theirs, "rep", [(i, (i + RING) % (2 * RING)) for i in range(2 * RING)])
    mine = lax.dynamic_slice_in_dim(share, start + half * HALF, HALF, 0)
    gu_mine, dn_mine, gain_mine = call(
        split_kernel,
        [((SHARE, 1, 2 * hid), f32), ((SHARE, 1, hid), f32), ((1, SHARE), f32)],
        (mine, theirs),
        kept=False,
    )
    return grad.T, gu_mine.transpose(1, 0, 2), dn_mine.transpose(1, 2, 0), gain_mine


def solution(mesh):
    placed = (
        P(("blk", "rep"), None),
        P(("blk", "rep"), None),
        P("blk", None, None),
        P("blk", None, None),
        P("blk", None),
    )
    return jax.shard_map(
        per_device,
        mesh=mesh,
        in_specs=placed,
        out_specs=(
            P(("blk", "rep"), None),
            P("blk", "rep", None),
            P("blk", None, "rep"),
            P("blk", "rep"),
        ),
        check_vma=False,
    )
```

```python
import functools

import jax
import jax.numpy as jnp
from jax import lax
from jax.experimental import pallas as pl
from jax.experimental.pallas import tpu as pltpu
from jax.sharding import PartitionSpec as P

SPANS = ((0, 512), (512, 768))
LANES = 128
SHARE = 36
RING = 8
HALF = 656
SLOT = 1328
SHORT = SLOT - 2

epsilon = 1e-05
bf16 = jnp.bfloat16
f32 = jnp.float32


def mul(a, b):
    return lax.dot_general(a, b, (((1,), (0,)), ((), ())), preferred_element_type=f32)


def mul_nt(a, b):
    return lax.dot_general(a, b, (((1,), (1,)), ((), ())), preferred_element_type=f32)


def column(row):
    return jnp.transpose(jnp.broadcast_to(row, (LANES, row.shape[1])))[:, :1]


def norm_parts(hidden):
    floated = hidden.astype(f32)
    inverse = lax.rsqrt(jnp.mean(floated * floated, axis=0, keepdims=True) + epsilon)
    return floated, inverse


def project(normed, gate_up_t):
    projected = mul(gate_up_t, normed)
    width = gate_up_t.shape[0] // 2
    gate_part = projected[:width]
    up_part = projected[width:]
    sig = jax.nn.sigmoid(gate_part)
    silu = gate_part * sig
    slope = up_part * sig * (1.0 + gate_part * (1.0 - sig))
    return (silu * up_part).astype(bf16), slope, silu


def back_through_norm(norm_grad, floated, inverse, outgrad, gain):
    product = norm_grad * floated * inverse
    size = product.shape[1]
    gain_term = functools.reduce(jnp.add, [product[:, i : i + LANES] for i in range(0, size, LANES)])
    scaled = norm_grad * gain
    inner = jnp.mean(scaled * floated, axis=0, keepdims=True)
    in_grad = outgrad.astype(f32) + inverse * (scaled - floated * (inverse * inverse * inner))
    return in_grad.astype(bf16), gain_term


def forward_part(hidden, gain, gu_t_ref, dn_t_ref, next_ref, normed_ref, act_ref, slope_ref, silu_ref):
    floated, inverse = norm_parts(hidden)
    normed = (floated * inverse * gain).astype(bf16)
    normed_ref[...] = normed
    activated, slope, silu = project(normed, gu_t_ref[...])
    act_ref[...] = activated
    slope_ref[...] = slope.astype(bf16)
    silu_ref[...] = silu.astype(bf16)
    next_ref[...] = (floated + mul(dn_t_ref[...], activated)).astype(bf16)


def first_kernel(span, *refs):
    sources, held, (gu_t_ref, dn_ref), outs, sems = refs[:4], refs[4:8], refs[8:10], refs[10:15], refs[15]
    copies = [pltpu.make_async_copy(src, dst, sems.at[i]) for i, (src, dst) in enumerate(zip(sources, held))]
    for copy in copies:
        copy.start()
    gain_ref, tok_ref, gu_ref, dn_t_ref = held
    copies[0].wait()
    copies[1].wait()
    copies[2].wait()
    gu_t_ref[...] = jnp.transpose(gu_ref[...])
    copies[3].wait()
    forward_part(tok_ref[:, span[0] : span[1]], column(gain_ref[...]), gu_t_ref, dn_t_ref, *outs)
    dn_ref[...] = jnp.transpose(dn_t_ref[...])


def next_kernel(span, gain_ref, tok_ref, gu_t_ref, dn_t_ref, *outs):
    forward_part(tok_ref[:, span[0] : span[1]], column(gain_ref[...]), gu_t_ref, dn_t_ref, *outs)


def turn_kernel(h_ref, out_ref, gu_t_ref, gu_ref, dn_ref, gain_ref, _, in_ref, normed_ref, act_ref, mixed_ref, term_ref):
    outgrad = out_ref[...]
    gain = column(gain_ref[...])
    floated, inverse = norm_parts(h_ref[...])
    normed = (floated * inverse * gain).astype(bf16)
    normed_ref[...] = normed
    activated, slope, silu = project(normed, gu_t_ref[...])
    act_ref[...] = activated
    act_grad = mul(dn_ref[...], outgrad)
    mixed = jnp.concatenate([(act_grad * slope).astype(bf16), (act_grad * silu).astype(bf16)], axis=0)
    mixed_ref[...] = mixed
    norm_grad = mul(gu_ref[...], mixed)
    in_ref[...], term_ref[...] = back_through_norm(norm_grad, floated, inverse, outgrad, gain)


def weight_kernel(*refs):
    count = len(SPANS)
    outs, normed, mixed, acts, terms = [refs[i * count : (i + 1) * count] for i in range(5)]
    gu_ref, dn_ref, gain_ref = refs[5 * count :]
    gu_ref[...] = functools.reduce(jnp.add, [mul_nt(a[...], b[...]) for a, b in zip(normed, mixed)])
    dn_ref[...] = functools.reduce(jnp.add, [mul_nt(a[...], b[...]) for a, b in zip(outs, acts)])
    gain_ref[...] = functools.reduce(jnp.add, [t[...] for t in terms])


def fill_slots(slots_ref, staged_ref, total_ref, sems, gu_sum, dn_sum, gain_sum):
    gain_sum = jnp.broadcast_to(gain_sum, (gain_sum.shape[0], LANES))
    columns = [x[:, i : i + LANES] for x in (gu_sum, dn_sum) for i in range(0, x.shape[1], LANES)]
    tail = HALF - SHARE * len(columns)
    own = lax.broadcasted_iota(jnp.int32, (SHARE, LANES), 0) == lax.broadcasted_iota(jnp.int32, (SHARE, LANES), 1)
    top = lax.broadcasted_iota(jnp.int32, (tail, LANES), 0) == 0
    copies = []
    for place in range(RING):
        for half in range(2):
            first = (half * RING + place) * SHARE
            rows = slice(first, first + SHARE)
            at = place * SLOT + half * HALF
            for column_block in columns:
                slots_ref[at : at + SHARE] = column_block[rows]
                at += SHARE
            gains = jnp.sum(jnp.where(own, gain_sum[rows], 0.0), axis=0, keepdims=True)
            slots_ref[at : at + tail] = jnp.where(top, gains, 0.0)
        low = place * SLOT
        if place < RING - 1:
            slots_ref[low + 2 * HALF : low + SLOT] = jnp.zeros((SLOT - 2 * HALF, LANES), f32)
            high = low + SLOT
        else:
            high = low + 2 * HALF
        staged_ref[low:high] = slots_ref[low:high].astype(bf16)
        copy = pltpu.make_async_copy(staged_ref.at[low:high], total_ref.at[low:high], sems.at[place])
        copy.start()
        copies.append(copy)
    for copy in copies:
        copy.wait()


def touch_kernel(out_ref, next_ref, seen_ref):
    seen_ref[...] = out_ref[:16, :LANES] + next_ref[:16, :LANES]


def backward_kernel(span, last, *refs):
    tok_ref, out_ref, slope_ref, silu_ref, normed_ref, act_ref, dn_ref, gu_ref, gain_ref = refs[:9]
    gu_sum_ref, dn_sum_ref, gain_sum_ref = refs[9:12]
    hid = dn_ref.shape[0]
    gain = column(gain_ref[...])
    outgrad = out_ref[...]
    act_grad = mul(dn_ref[...], outgrad)
    mixed = jnp.concatenate(
        [
            (act_grad * slope_ref[...].astype(f32)).astype(bf16),
            (act_grad * silu_ref[...].astype(f32)).astype(bf16),
        ],
        axis=0,
    )
    floated, inverse = norm_parts(tok_ref[:, span[0] : span[1]])
    norm_grad = mul(gu_ref[...], mixed)
    in_grad, term = back_through_norm(norm_grad, floated, inverse, outgrad, gain)
    gu_sum = gu_sum_ref[...] + mul_nt(normed_ref[...], mixed)
    dn_sum = dn_sum_ref[...] + mul_nt(outgrad, act_ref[...])
    gain_sum = gain_sum_ref[...] + term
    if last:
        before_ref, grad_ref, total_ref, slots_ref, staged_ref, sems = refs[12:]
        grad_ref[:, : span[0]] = before_ref[...]
        grad_ref[:, span[0] : span[1]] = in_grad
        gain_sum = jnp.sum(gain_sum, axis=1, keepdims=True)
        fill_slots(slots_ref, staged_ref, total_ref, sems, gu_sum, dn_sum, gain_sum)
    else:
        in_ref, gu_out, dn_out, gain_out = refs[12:]
        in_ref[...] = in_grad
        gu_out[...] = gu_sum
        dn_out[...] = dn_sum
        gain_out[...] = gain_sum


def call(kernel, outs, args, flops, aliases={}, kept=True, scratch=(), free=0, moved=False):
    shaped = pltpu.VMEM if kept else jax.ShapeDtypeStruct
    inside, outside = pl.BlockSpec(memory_space=pltpu.VMEM), pl.BlockSpec(memory_space=pltpu.HBM)
    held = len(outs) - free
    return pl.pallas_call(
        kernel,
        out_shape=[shaped(*o) for o in outs[:held]] + [pltpu.HBM(*o) for o in outs[held:]],
        in_specs=[outside if moved else inside] * len(args),
        out_specs=[inside] * held + [outside] * free,
        input_output_aliases=aliases,
        scratch_shapes=scratch,
        compiler_params=pltpu.CompilerParams(vmem_limit_bytes=28 * 2**20),
        cost_estimate=pl.CostEstimate(flops=flops, bytes_accessed=flops // 200, transcendentals=0),
    )(*[pltpu.with_memory_space_constraint(a, pltpu.HBM if moved else pltpu.VMEM) for a in args])


def passed_along(x, axis, by):
    peers = lax.axis_size(axis)
    return lax.ppermute(x, axis, [(i, (i + by) % peers) for i in range(peers)])


def split_kernel(in_ref, other_ref, gu_ref, dn_ref, gain_ref):
    at = 0
    got = in_ref[...].astype(f32) + other_ref[...].astype(f32)
    for ref in (gu_ref, dn_ref):
        for i in range(0, ref.shape[2], LANES):
            ref[:, :, i : i + LANES] = got[at : at + SHARE][:, None, :]
            at += SHARE
    gain_ref[...] = got[at : at + 1, :SHARE]


def per_device(tokens, cotangent, gate_up, down_proj, norm_gain):
    tok, cot = tokens.T, cotangent.T
    gu, dn_t, gain = gate_up[0], down_proj[0].T, norm_gain
    width, rows = tok.shape
    hid = dn_t.shape[1]
    length = RING * SHORT
    unit = 4 * width * hid
    cots = [passed_along(cot[:, lo:hi], "blk", 1) for lo, hi in SPANS]
    kept, nexts = [], []
    for i, (lo, hi) in enumerate(SPANS):
        shapes = [((n, hi - lo), bf16) for n in (width, width, hid, hid, hid)]
        cost = 3 * unit * (hi - lo)
        if i == 0:
            args = (gain, tok, gu, dn_t)
            held = [(a.shape, a.dtype) for a in args] + [((2 * hid, width), bf16), ((hid, width), bf16)]
            gain, tok, gu, dn_t, gu_t, dn, *parts = call(
                functools.partial(first_kernel, (lo, hi)),
                held + shapes,
                args,
                cost,
                scratch=[pltpu.SemaphoreType.DMA((len(args),))],
                moved=True,
            )
        else:
            parts = call(functools.partial(next_kernel, (lo, hi)), shapes, (gain, tok, gu_t, dn_t), cost)
        nexts.append(parts[0])
        kept.append(parts[1:])
    hiddens = [passed_along(nxt, "blk", 1) for nxt in nexts]
    turned, returned = [], []
    (after,) = call(touch_kernel, [((16, LANES), bf16)], (cots[0], nexts[-1]), unit)
    for i, (lo, hi) in enumerate(SPANS):
        n = hi - lo
        in_grad, *parts = call(
            turn_kernel,
            [((width, n), bf16)] * 2 + [((hid, n), bf16), ((2 * hid, n), bf16), ((width, LANES), f32)],
            (hiddens[i], cots[i], gu_t, gu, dn, gain, after),
            5 * unit * n,
        )
        after = in_grad
        turned.append(parts)
        returned.append(passed_along(in_grad, "blk", -1))
    sums_shape = [((width, 2 * hid), f32), ((width, hid), f32), ((width, LANES), f32)]
    sums = call(
        weight_kernel,
        sums_shape,
        cots + [part[i] for i in (0, 2, 1, 3) for part in turned],
        3 * unit * rows,
    )
    before = None
    for (lo, hi), back, (normed, act, slope, silu) in zip(SPANS, returned, kept):
        last = hi == rows
        args = (tok, back, slope, silu, normed, act, dn, gu, gain, *sums)
        kernel = functools.partial(backward_kernel, (lo, hi), last)
        if last:
            shapes = [((width, rows), bf16), ((length, LANES), bf16)]
            scratch = [pltpu.VMEM((length, LANES), f32), pltpu.VMEM((length, LANES), bf16), pltpu.SemaphoreType.DMA((RING,))]
            grad, total = call(kernel, shapes, (*args, before), 6 * unit * (hi - lo), scratch=scratch, free=1)
        else:
            before, *sums = call(
                kernel, [((width, hi - lo), bf16)] + sums_shape, args, 6 * unit * (hi - lo), {9: 1, 10: 2, 11: 3}
            )
    rings = [[half * RING + place for place in range(RING)] for half in range(2)]
    share = lax.psum_scatter(total, "rep", scatter_dimension=0, axis_index_groups=rings, tiled=True)
    share = lax.optimization_barrier(share)
    at = lax.axis_index("rep")
    half, start = at // RING, (at % RING) * (SLOT - SHORT)
    theirs = lax.dynamic_slice_in_dim(share, start + (1 - half) * HALF, HALF, 0)
    theirs = lax.ppermute(theirs, "rep", [(i, (i + RING) % (2 * RING)) for i in range(2 * RING)])
    mine = lax.dynamic_slice_in_dim(share, start + half * HALF, HALF, 0)
    gu_mine, dn_mine, gain_mine = call(
        split_kernel,
        [((SHARE, 1, 2 * hid), f32), ((SHARE, 1, hid), f32), ((1, SHARE), f32)],
        (mine, theirs),
        unit,
        kept=False,
    )
    return grad.T, gu_mine.transpose(1, 0, 2), dn_mine.transpose(1, 2, 0), gain_mine


def solution(mesh):
    placed = (
        P(("blk", "rep"), None),
        P(("blk", "rep"), None),
        P("blk", None, None),
        P("blk", None, None),
        P("blk", None),
    )
    return jax.shard_map(
        per_device,
        mesh=mesh,
        in_specs=placed,
        out_specs=(
            P(("blk", "rep"), None),
            P("blk", "rep", None),
            P("blk", None, "rep"),
            P("blk", "rep"),
        ),
        check_vma=False,
    )
```

```python
import functools

import jax
import jax.numpy as jnp
from jax import lax
from jax.experimental import pallas as pl
from jax.experimental.pallas import tpu as pltpu
from jax.sharding import PartitionSpec as P

SPANS = ((0, 512), (512, 768))
LANES = 128
SHARE = 36
RING = 8
HALF = 656
SLOT = 1328
SHORT = SLOT - 2

epsilon = 1e-05
bf16 = jnp.bfloat16
f32 = jnp.float32


def mul(a, b):
    return lax.dot_general(a, b, (((1,), (0,)), ((), ())), preferred_element_type=f32)


def mul_nt(a, b):
    return lax.dot_general(a, b, (((1,), (1,)), ((), ())), preferred_element_type=f32)


def column(row):
    return jnp.transpose(jnp.broadcast_to(row, (LANES, row.shape[1])))[:, :1]


def norm_parts(hidden):
    floated = hidden.astype(f32)
    inverse = lax.rsqrt(jnp.mean(floated * floated, axis=0, keepdims=True) + epsilon)
    return floated, inverse


def project(normed, gate_up_t):
    projected = mul(gate_up_t, normed)
    width = gate_up_t.shape[0] // 2
    gate_part = projected[:width]
    up_part = projected[width:]
    sig = jax.nn.sigmoid(gate_part)
    silu = gate_part * sig
    slope = up_part * sig * (1.0 + gate_part * (1.0 - sig))
    return (silu * up_part).astype(bf16), slope, silu


def back_through_norm(norm_grad, floated, inverse, outgrad, gain):
    product = norm_grad * floated * inverse
    size = product.shape[1]
    gain_term = functools.reduce(jnp.add, [product[:, i : i + LANES] for i in range(0, size, LANES)])
    scaled = norm_grad * gain
    inner = jnp.mean(scaled * floated, axis=0, keepdims=True)
    in_grad = outgrad.astype(f32) + inverse * (scaled - floated * (inverse * inverse * inner))
    return in_grad.astype(bf16), gain_term


def forward_part(hidden, gain, gu_t_ref, dn_t_ref, next_ref, normed_ref, act_ref, slope_ref, silu_ref):
    floated, inverse = norm_parts(hidden)
    normed = (floated * inverse * gain).astype(bf16)
    normed_ref[...] = normed
    activated, slope, silu = project(normed, gu_t_ref[...])
    act_ref[...] = activated
    slope_ref[...] = slope.astype(bf16)
    silu_ref[...] = silu.astype(bf16)
    next_ref[...] = (floated + mul(dn_t_ref[...], activated)).astype(bf16)


def first_kernel(span, *refs):
    sources, held, (gu_t_ref, dn_ref), outs, sems = refs[:4], refs[4:8], refs[8:10], refs[10:15], refs[15]
    copies = [pltpu.make_async_copy(src, dst, sems.at[i]) for i, (src, dst) in enumerate(zip(sources, held))]
    for copy in copies:
        copy.start()
    gain_ref, tok_ref, gu_ref, dn_t_ref = held
    copies[0].wait()
    copies[1].wait()
    copies[2].wait()
    gu_t_ref[...] = jnp.transpose(gu_ref[...])
    copies[3].wait()
    forward_part(tok_ref[:, span[0] : span[1]], column(gain_ref[...]), gu_t_ref, dn_t_ref, *outs)
    dn_ref[...] = jnp.transpose(dn_t_ref[...])


def next_kernel(span, gain_ref, tok_ref, gu_t_ref, dn_t_ref, *outs):
    forward_part(tok_ref[:, span[0] : span[1]], column(gain_ref[...]), gu_t_ref, dn_t_ref, *outs)


def turn_kernel(h_ref, out_ref, gu_t_ref, gu_ref, dn_ref, gain_ref, _, in_ref, normed_ref, act_ref, mixed_ref, term_ref):
    outgrad = out_ref[...]
    gain = column(gain_ref[...])
    floated, inverse = norm_parts(h_ref[...])
    normed = (floated * inverse * gain).astype(bf16)
    normed_ref[...] = normed
    activated, slope, silu = project(normed, gu_t_ref[...])
    act_ref[...] = activated
    act_grad = mul(dn_ref[...], outgrad)
    mixed = jnp.concatenate([(act_grad * slope).astype(bf16), (act_grad * silu).astype(bf16)], axis=0)
    mixed_ref[...] = mixed
    norm_grad = mul(gu_ref[...], mixed)
    in_ref[...], term_ref[...] = back_through_norm(norm_grad, floated, inverse, outgrad, gain)


def weight_kernel(out_ref, normed_ref, mixed_ref, act_ref, term_ref, *refs):
    before, (gu_ref, dn_ref, gain_ref) = refs[:-3], refs[-3:]
    sums = [mul_nt(normed_ref[...], mixed_ref[...]), mul_nt(out_ref[...], act_ref[...]), term_ref[...]]
    if before:
        sums = [ref[...] + x for ref, x in zip(before, sums)]
    gu_ref[...], dn_ref[...], gain_ref[...] = sums


def fill_slots(slots_ref, staged_ref, total_ref, sems, gu_sum, dn_sum, gain_sum):
    gain_sum = jnp.broadcast_to(gain_sum, (gain_sum.shape[0], LANES))
    columns = [x[:, i : i + LANES] for x in (gu_sum, dn_sum) for i in range(0, x.shape[1], LANES)]
    tail = HALF - SHARE * len(columns)
    own = lax.broadcasted_iota(jnp.int32, (SHARE, LANES), 0) == lax.broadcasted_iota(jnp.int32, (SHARE, LANES), 1)
    top = lax.broadcasted_iota(jnp.int32, (tail, LANES), 0) == 0
    copies = []
    for place in range(RING):
        for half in range(2):
            first = (half * RING + place) * SHARE
            rows = slice(first, first + SHARE)
            at = place * SLOT + half * HALF
            for column_block in columns:
                slots_ref[at : at + SHARE] = column_block[rows]
                at += SHARE
            gains = jnp.sum(jnp.where(own, gain_sum[rows], 0.0), axis=0, keepdims=True)
            slots_ref[at : at + tail] = jnp.where(top, gains, 0.0)
        low = place * SLOT
        if place < RING - 1:
            slots_ref[low + 2 * HALF : low + SLOT] = jnp.zeros((SLOT - 2 * HALF, LANES), f32)
            high = low + SLOT
        else:
            high = low + 2 * HALF
        staged_ref[low:high] = slots_ref[low:high].astype(bf16)
        copy = pltpu.make_async_copy(staged_ref.at[low:high], total_ref.at[low:high], sems.at[place])
        copy.start()
        copies.append(copy)
    for copy in copies:
        copy.wait()


def touch_kernel(out_ref, next_ref, seen_ref):
    seen_ref[...] = out_ref[:16, :LANES] + next_ref[:16, :LANES]


def backward_kernel(span, last, *refs):
    tok_ref, out_ref, slope_ref, silu_ref, normed_ref, act_ref, dn_ref, gu_ref, gain_ref = refs[:9]
    gu_sum_ref, dn_sum_ref, gain_sum_ref = refs[9:12]
    hid = dn_ref.shape[0]
    gain = column(gain_ref[...])
    outgrad = out_ref[...]
    act_grad = mul(dn_ref[...], outgrad)
    mixed = jnp.concatenate(
        [
            (act_grad * slope_ref[...].astype(f32)).astype(bf16),
            (act_grad * silu_ref[...].astype(f32)).astype(bf16),
        ],
        axis=0,
    )
    floated, inverse = norm_parts(tok_ref[:, span[0] : span[1]])
    norm_grad = mul(gu_ref[...], mixed)
    in_grad, term = back_through_norm(norm_grad, floated, inverse, outgrad, gain)
    gu_sum = gu_sum_ref[...] + mul_nt(normed_ref[...], mixed)
    dn_sum = dn_sum_ref[...] + mul_nt(outgrad, act_ref[...])
    gain_sum = gain_sum_ref[...] + term
    if last:
        before_ref, grad_ref, total_ref, slots_ref, staged_ref, sems = refs[12:]
        grad_ref[:, : span[0]] = before_ref[...]
        grad_ref[:, span[0] : span[1]] = in_grad
        gain_sum = jnp.sum(gain_sum, axis=1, keepdims=True)
        fill_slots(slots_ref, staged_ref, total_ref, sems, gu_sum, dn_sum, gain_sum)
    else:
        in_ref, gu_out, dn_out, gain_out = refs[12:]
        in_ref[...] = in_grad
        gu_out[...] = gu_sum
        dn_out[...] = dn_sum
        gain_out[...] = gain_sum


def call(kernel, outs, args, flops, aliases={}, kept=True, scratch=(), free=0, moved=False):
    shaped = pltpu.VMEM if kept else jax.ShapeDtypeStruct
    inside, outside = pl.BlockSpec(memory_space=pltpu.VMEM), pl.BlockSpec(memory_space=pltpu.HBM)
    held = len(outs) - free
    return pl.pallas_call(
        kernel,
        out_shape=[shaped(*o) for o in outs[:held]] + [pltpu.HBM(*o) for o in outs[held:]],
        in_specs=[outside if moved else inside] * len(args),
        out_specs=[inside] * held + [outside] * free,
        input_output_aliases=aliases,
        scratch_shapes=scratch,
        compiler_params=pltpu.CompilerParams(vmem_limit_bytes=28 * 2**20),
        cost_estimate=pl.CostEstimate(flops=flops, bytes_accessed=flops // 200, transcendentals=0),
    )(*[pltpu.with_memory_space_constraint(a, pltpu.HBM if moved else pltpu.VMEM) for a in args])


def passed_along(x, axis, by):
    peers = lax.axis_size(axis)
    return lax.ppermute(x, axis, [(i, (i + by) % peers) for i in range(peers)])


def split_kernel(in_ref, other_ref, gu_ref, dn_ref, gain_ref):
    at = 0
    got = in_ref[...].astype(f32) + other_ref[...].astype(f32)
    for ref in (gu_ref, dn_ref):
        for i in range(0, ref.shape[2], LANES):
            ref[:, :, i : i + LANES] = got[at : at + SHARE][:, None, :]
            at += SHARE
    gain_ref[...] = got[at : at + 1, :SHARE]


def per_device(tokens, cotangent, gate_up, down_proj, norm_gain):
    tok, cot = tokens.T, cotangent.T
    gu, dn_t, gain = gate_up[0], down_proj[0].T, norm_gain
    width, rows = tok.shape
    hid = dn_t.shape[1]
    length = RING * SHORT
    unit = 4 * width * hid
    cots = [passed_along(cot[:, lo:hi], "blk", 1) for lo, hi in SPANS]
    kept, nexts = [], []
    for i, (lo, hi) in enumerate(SPANS):
        shapes = [((n, hi - lo), bf16) for n in (width, width, hid, hid, hid)]
        cost = 3 * unit * (hi - lo)
        if i == 0:
            args = (gain, tok, gu, dn_t)
            held = [(a.shape, a.dtype) for a in args] + [((2 * hid, width), bf16), ((hid, width), bf16)]
            gain, tok, gu, dn_t, gu_t, dn, *parts = call(
                functools.partial(first_kernel, (lo, hi)),
                held + shapes,
                args,
                cost,
                scratch=[pltpu.SemaphoreType.DMA((len(args),))],
                moved=True,
            )
        else:
            parts = call(functools.partial(next_kernel, (lo, hi)), shapes, (gain, tok, gu_t, dn_t), cost)
        nexts.append(parts[0])
        kept.append(parts[1:])
    hiddens = [passed_along(nxt, "blk", 1) for nxt in nexts]
    sums_shape = [((width, 2 * hid), f32), ((width, hid), f32), ((width, LANES), f32)]
    sums, returned = [], []
    (after,) = call(touch_kernel, [((16, LANES), bf16)], (cots[0], nexts[-1]), unit)
    for i, (lo, hi) in enumerate(SPANS):
        n = hi - lo
        in_grad, normed, act, mixed, term = call(
            turn_kernel,
            [((width, n), bf16)] * 2 + [((hid, n), bf16), ((2 * hid, n), bf16), ((width, LANES), f32)],
            (hiddens[i], cots[i], gu_t, gu, dn, gain, after),
            5 * unit * n,
        )
        args = (cots[i], normed, mixed, act, term, *sums)
        sums = call(weight_kernel, sums_shape, args, 3 * unit * n, {5: 0, 6: 1, 7: 2} if sums else {})
        after = sums[-1]
        returned.append(passed_along(in_grad, "blk", -1))
    before = None
    for (lo, hi), back, (normed, act, slope, silu) in zip(SPANS, returned, kept):
        last = hi == rows
        args = (tok, back, slope, silu, normed, act, dn, gu, gain, *sums)
        kernel = functools.partial(backward_kernel, (lo, hi), last)
        if last:
            shapes = [((width, rows), bf16), ((length, LANES), bf16)]
            scratch = [pltpu.VMEM((length, LANES), f32), pltpu.VMEM((length, LANES), bf16), pltpu.SemaphoreType.DMA((RING,))]
            grad, total = call(kernel, shapes, (*args, before), 6 * unit * (hi - lo), scratch=scratch, free=1)
        else:
            before, *sums = call(
                kernel, [((width, hi - lo), bf16)] + sums_shape, args, 6 * unit * (hi - lo), {9: 1, 10: 2, 11: 3}
            )
    rings = [[half * RING + place for place in range(RING)] for half in range(2)]
    share = lax.psum_scatter(total, "rep", scatter_dimension=0, axis_index_groups=rings, tiled=True)
    share = lax.optimization_barrier(share)
    at = lax.axis_index("rep")
    half, start = at // RING, (at % RING) * (SLOT - SHORT)
    theirs = lax.dynamic_slice_in_dim(share, start + (1 - half) * HALF, HALF, 0)
    theirs = lax.ppermute(theirs, "rep", [(i, (i + RING) % (2 * RING)) for i in range(2 * RING)])
    mine = lax.dynamic_slice_in_dim(share, start + half * HALF, HALF, 0)
    gu_mine, dn_mine, gain_mine = call(
        split_kernel,
        [((SHARE, 1, 2 * hid), f32), ((SHARE, 1, hid), f32), ((1, SHARE), f32)],
        (mine, theirs),
        unit,
        kept=False,
    )
    return grad.T, gu_mine.transpose(1, 0, 2), dn_mine.transpose(1, 2, 0), gain_mine


def solution(mesh):
    placed = (
        P(("blk", "rep"), None),
        P(("blk", "rep"), None),
        P("blk", None, None),
        P("blk", None, None),
        P("blk", None),
    )
    return jax.shard_map(
        per_device,
        mesh=mesh,
        in_specs=placed,
        out_specs=(
            P(("blk", "rep"), None),
            P("blk", "rep", None),
            P("blk", None, "rep"),
            P("blk", "rep"),
        ),
        check_vma=False,
    )
```
